32 devices in a mesh: shard: 8 (over z, x), ctx: 2 (over y), tp: 2 (over core).
Axes of the slice: x: 2, y: 2, z: 4, core: 2. Of those that a mesh axis runs over, the one named last changes fastest.
Arguments:
- tokens: bfloat16 [16, 1024, 1024], P('shard', 'ctx'), may hold values from -6 to 6
- segments: int32 [16, 1024], P('shard'), may hold values from 0 to 3, as said below
- cotangent: bfloat16 [16, 1024, 1024], P('shard', 'ctx'), may hold values from -6 to 6
- mix_gain: float32 [1024], replicated, may hold values from 0.5 to 1.5
- ffn_gain: float32 [1024], replicated, may hold values from 0.5 to 1.5
- ssm_gate: bfloat16 [1024, 1536], P(('shard', 'ctx'), 'tp'), may hold values from -0.1875 to 0.1875
- ssm_input: bfloat16 [1024, 1536], P(('shard', 'ctx'), 'tp'), may hold values from -0.1875 to 0.1875
- ssm_state: bfloat16 [1024, 256], P(('shard', 'ctx')), may hold values from -0.1875 to 0.1875
- ssm_step: bfloat16 [1024, 24], P(('shard', 'ctx'), 'tp'), may hold values from -0.1875 to 0.1875
- attn_query: bfloat16 [1024, 512], P(('shard', 'ctx'), 'tp'), may hold values from -0.1875 to 0.1875
- attn_keyval: bfloat16 [1024, 2, 128], P(('shard', 'ctx'), 'tp'), may hold values from -0.1875 to 0.1875
- ssm_out: bfloat16 [1536, 1024], P('tp', ('shard', 'ctx')), may hold values from -0.109375 to 0.109375
- attn_out: bfloat16 [512, 1024], P('tp', ('shard', 'ctx')), may hold values from -3 to 3
- ffn_gate: bfloat16 [1024, 2048], P(('shard', 'ctx'), 'tp'), may hold values from -0.1875 to 0.1875
- ffn_up: bfloat16 [1024, 2048], P(('shard', 'ctx'), 'tp'), may hold values from -0.1875 to 0.1875
- ffn_down: bfloat16 [2048, 1024], P('tp', ('shard', 'ctx')), may hold values from -0.125 to 0.125
- conv_input: float32 [4, 1536], P(None, 'tp'), may hold values from -2.5 to 2.5
- conv_state: float32 [4, 256], replicated, may hold values from -2.5 to 2.5
- step_bias: float32 [24], P('tp'), may hold values from -1.5 to 0.5
- decay_rate: float32 [24], P('tp'), may hold values from 0.0009765625 to 0.05
Outputs:
- layer_out: bfloat16 [16, 1024, 1024], P('shard', 'ctx')
- grad_tokens: float32 [16, 1024, 1024], P('shard', 'ctx')
- grad_mix_gain: float32 [1024], replicated
- grad_ffn_gain: float32 [1024], replicated
- grad_ssm_gate: float32 [1024, 1536], P(('shard', 'ctx'), 'tp')
- grad_ssm_input: float32 [1024, 1536], P(('shard', 'ctx'), 'tp')
- grad_ssm_state: float32 [1024, 256], P(('shard', 'ctx'))
- grad_ssm_step: float32 [1024, 24], P(('shard', 'ctx'), 'tp')
- grad_attn_query: float32 [1024, 512], P(('shard', 'ctx'), 'tp')
- grad_attn_keyval: float32 [1024, 2, 128], P(('shard', 'ctx'), 'tp')
- grad_ssm_out: float32 [1536, 1024], P('tp', ('shard', 'ctx'))
- grad_attn_out: float32 [512, 1024], P('tp', ('shard', 'ctx'))
- grad_ffn_gate: float32 [1024, 2048], P(('shard', 'ctx'), 'tp')
- grad_ffn_up: float32 [1024, 2048], P(('shard', 'ctx'), 'tp')
- grad_ffn_down: float32 [2048, 1024], P('tp', ('shard', 'ctx'))
- grad_conv_input: float32 [4, 1536], P(None, 'tp')
- grad_conv_state: float32 [4, 256], replicated
- grad_step_bias: float32 [24], P('tp')
- grad_decay_rate: float32 [24], P('tp')
The draws below stay inside these ranges and needn't reach their ends.
Inputs may be any that keep to these rules, and one draw needn't show every extreme that they name: `segments`: along each sequence the ids start at 0 and never fall; of the 2 sequences at each index of shard, one keeps id 0 up to position 768 or later.
All inputs are finite; a program needn't handle non-finite values.
Results may differ from the reference program's by a relative error of at most 0.019.
Values may be sent and summed in bfloat16 or wider, within the bound.
A program may use at most 192 MiB of HBM per device.

```python
import math
from functools import partial
import jax
import jax.numpy as jnp
from jax import lax

D = 1024
H = 24
P_SIZE = 64
N = 128
K = 4
QH = 8
KVH = 2
HD = 64
FF = 2048
LEN = 1024
DI = 1536
SPAN = 512
SEQS = 2
SEQ_ALL = 16
N_SHARD = 8
N_CTX = 2


def draw_segments(key, part):
    key = jax.random.fold_in(key, 11)
    key_bounds, key_pick, key_late = jax.random.split(key, 3)
    bounds = jax.random.randint(key_bounds, (SEQ_ALL, 3), 1, LEN)
    picked = jax.random.randint(key_pick, (N_SHARD,), 0, SEQS)
    row_ids = jnp.arange(SEQ_ALL)
    chosen = row_ids % SEQS == jnp.repeat(picked, SEQS)
    late = jax.random.randint(key_late, (SEQ_ALL, 3), LEN - SPAN // 2, LEN)
    bounds = jnp.where(chosen[:, None], late, bounds)
    ordinal = jnp.arange(LEN)
    return jnp.sum((ordinal[None, :, None] >= bounds[:, None, :]).astype(jnp.int32), axis=2).astype(jnp.int32)


def block_levels(rng, extent, cuts, low, top_value):
    gain, own = 1.0, jax.random.fold_in(rng, 6)
    for position, parts in cuts:
        draws = jnp.exp(jax.random.uniform(jax.random.fold_in(own, position), (parts,), jnp.float32, low / len(cuts), top_value / len(cuts)))
        gain = gain * jnp.repeat(draws, extent[position] // parts).reshape([-1 if axis == position else 1 for axis in range(len(extent))])
    return gain


def centred(own_key, dims, width, bound, cuts=(), kind=jnp.bfloat16):
    array = jax.random.normal(own_key, dims, jnp.float32) * width
    if len(cuts) > 0:
        array = block_levels(own_key, dims, cuts, -0.22, 0.18) * array
    return jnp.clip(array, min=-bound, max=bound).astype(kind)


def setup_inputs(seed: int = 0) -> dict:
    seeds = jax.random.split(jax.random.key(seed), 21)
    tokens = centred(seeds[0], (SEQ_ALL, LEN, D), 1.0, 6.0, ((0, 8), (1, 2)))
    segments = draw_segments(jax.random.fold_in(seeds[20], 71), 0)
    cotangent = centred(seeds[2], (SEQ_ALL, LEN, D), 1.0, 6.0, ((0, 8), (1, 2)))
    mix_gain = jnp.clip(1.0 + 0.1 * jax.random.normal(seeds[3], (D,), jnp.float32), 0.5, 1.5)
    ffn_gain = jnp.clip(1.0 + 0.1 * jax.random.normal(seeds[4], (D,), jnp.float32), 0.5, 1.5)
    ssm_gate = centred(seeds[5], (D, DI), D ** -0.5, 0.1875, ((0, 16), (1, 2)))
    ssm_input = centred(seeds[6], (D, DI), D ** -0.5, 0.1875, ((0, 16), (1, 2)))
    ssm_state = centred(seeds[7], (D, 2 * N), D ** -0.5, 0.1875, ((0, 16),))
    ssm_step = centred(seeds[8], (D, H), D ** -0.5, 0.1875, ((0, 16), (1, 2)))
    attn_query = centred(seeds[9], (D, QH * HD), D ** -0.5, 0.1875, ((0, 16), (1, 2)))
    attn_keyval = centred(seeds[10], (D, KVH, 2 * HD), D ** -0.5, 0.1875, ((0, 16), (1, 2)))
    ssm_out = centred(seeds[11], (DI, D), (DI * 2) ** -0.5, 0.109375, ((0, 2), (1, 16)))
    attn_out = centred(seeds[12], (QH * HD, D), (max(1, QH * HD * 8 // LEN)) ** -0.5, 3.0, ((0, 2), (1, 16)))
    ffn_gate = centred(seeds[13], (D, FF), D ** -0.5, 0.1875, ((0, 16), (1, 2)))
    ffn_up = centred(seeds[14], (D, FF), D ** -0.5, 0.1875, ((0, 16), (1, 2)))
    ffn_down = centred(seeds[15], (FF, D), FF ** -0.5, 0.125, ((0, 2), (1, 16)))
    conv_input = centred(seeds[16], (K, DI), 0.5, 2.5, ((1, 2),), jnp.float32)
    conv_state = centred(seeds[17], (K, 2 * N), 0.5, 2.5, (), jnp.float32)
    step_bias = jnp.clip(-1.5 + 2.0 * jax.random.uniform(seeds[18], (H,), jnp.float32) ** block_levels(seeds[18], (H,), ((0, 2),), -0.2, 0.2), -1.5, 0.5)
    decay_rate = jnp.clip(jnp.exp(math.log(0.05) - 3.9357395 * jax.random.uniform(seeds[19], (H,), jnp.float32) ** block_levels(seeds[19], (H,), ((0, 2),), -0.2, 0.2)), 0.0009765625, 0.05)
    return dict(tokens=tokens, segments=segments, cotangent=cotangent, mix_gain=mix_gain, ffn_gain=ffn_gain, ssm_gate=ssm_gate, ssm_input=ssm_input, ssm_state=ssm_state, ssm_step=ssm_step, attn_query=attn_query, attn_keyval=attn_keyval, ssm_out=ssm_out, attn_out=attn_out, ffn_gate=ffn_gate, ffn_up=ffn_up, ffn_down=ffn_down, conv_input=conv_input, conv_state=conv_state, step_bias=step_bias, decay_rate=decay_rate)


epsilon = 1e-05
highest = lax.Precision.HIGHEST

@jax.custom_vjp
def low(v):
    return lax.optimization_barrier(v.astype(jnp.bfloat16)).astype(jnp.float32)

@jax.custom_vjp
def low_back(v):
    return v

def low_keep(v):
    return (low(v), None)

def low_pass(kept, grad):
    return (grad,)

def back_keep(v):
    return (v, None)

def back_low(kept, grad):
    return (low(grad),)
low.defvjp(low_keep, low_pass)
low_back.defvjp(back_keep, back_low)

def product(left_side, right_side):
    return jnp.dot(left_side, right_side, precision=highest, preferred_element_type=jnp.float32)

def rms_norm(values, norm_gain):
    inv_rms = lax.rsqrt(lax.optimization_barrier(jnp.mean(values * values, axis=-1, keepdims=True)) + epsilon)
    return values * inv_rms * norm_gain

def rotary_tables(positions, head_dim):
    half_dim = head_dim // 2
    frequency = 10000.0 ** (-2.0 * jnp.arange(half_dim, dtype=jnp.float32) / head_dim)
    angles = positions.astype(jnp.float32)[:, None] * frequency[None, :]
    return (jnp.cos(angles), jnp.sin(angles))

def rotate(values, cos_table, sin_table):
    half_dim = values.shape[-1] // 2
    first_half = values[..., :half_dim]
    second_half = values[..., half_dim:]
    return jnp.concatenate([first_half * cos_table - second_half * sin_table, second_half * cos_table + first_half * sin_table], axis=-1)

def span_states(inner_act, input_mat, step_size, decay_rate, seg_part, seg_before):
    cumulative = jnp.cumsum(-step_size * decay_rate, axis=1)
    at_end = (seg_part == seg_part[:, -1:])[..., None]
    tail_decay = jnp.where(at_end, jnp.exp(cumulative[:, -1:, :] - cumulative), 0.0)
    weighted = inner_act * (tail_decay * step_size)[..., None]
    states = jnp.einsum('stha,stn->shan', weighted, input_mat, precision=highest)
    linked = (seg_part[:, -1] == seg_before)[:, None]
    linkage = jnp.where(linked, jnp.exp(cumulative[:, -1, :]), 0.0)
    return (states, linkage, cumulative)

def span_outputs(inner_act, input_mat, output_mat, step_size, seg_part, seg_before, cumulative, incoming):
    length = inner_act.shape[1]
    ordinal = jnp.arange(length)
    allowed = (seg_part[:, :, None] == seg_part[:, None, :]) & (ordinal[:, None] >= ordinal[None, :])[None]
    allowed = allowed[..., None]
    spread = cumulative[:, :, None, :] - cumulative[:, None, :, :]
    decays = jnp.where(allowed, jnp.exp(jnp.where(allowed, spread, 0.0)), 0.0)
    intersection = jnp.einsum('stn,sun->stu', output_mat, input_mat, precision=highest)
    mixing = intersection[..., None] * decays * step_size[:, None, :, :]
    local_part = jnp.einsum('stuh,suha->stha', mixing, inner_act, precision=highest)
    entrance = jnp.where((seg_part == seg_before[:, None])[..., None], jnp.exp(cumulative), 0.0)
    carried = jnp.einsum('shan,stn->stha', incoming, output_mat, precision=highest) * entrance[..., None]
    return local_part + carried

def sequence_mixer(sequence, decay_rate):
    inner_act, input_mat, output_mat, step_size, seg_row = sequence
    pieces = (inner_act.reshape(N_CTX, 1, SPAN, H, P_SIZE), input_mat.reshape(N_CTX, 1, SPAN, N), output_mat.reshape(N_CTX, 1, SPAN, N), step_size.reshape(N_CTX, 1, SPAN, H), seg_row.reshape(N_CTX, 1, SPAN))

    def advance(running, block_part):
        incoming, seg_before = running
        act_part, in_part, out_part, step_part, seg_part = block_part
        states, linkage, cumulative = span_states(act_part, in_part, step_part, decay_rate, seg_part, seg_before)
        result = span_outputs(act_part, in_part, out_part, step_part, seg_part, seg_before, cumulative, incoming)
        return ((linkage[..., None, None] * incoming + states, seg_part[:, -1]), result)
    start_state = (jnp.zeros((1, H, P_SIZE, N), jnp.float32), jnp.full((1,), -1, jnp.int32))
    unused_state, results = lax.scan(jax.checkpoint(advance), start_state, pieces)
    return results.reshape(LEN, H, P_SIZE)

def sequence_attention(sequence):
    queries, keyval, seg_row = sequence
    grouped = queries.reshape(LEN, KVH, QH // KVH, HD)
    scores = jnp.einsum('tgjd,ugd->gjtu', grouped, keyval[..., :HD], precision=highest) * HD ** (-0.5)
    scores = low_back(scores)
    ordinal = jnp.arange(LEN)
    allowed = (ordinal[:, None] >= ordinal[None, :]) & (seg_row[:, None] == seg_row[None, :])
    scores = jnp.where(allowed, scores, -1e+30)
    largest = lax.optimization_barrier(jnp.max(scores, axis=-1, keepdims=True))
    log_total = largest + jnp.log(lax.optimization_barrier(jnp.sum(jnp.exp(scores - largest), axis=-1, keepdims=True)))
    attn_probs = low(jnp.exp(scores - log_total))
    attended = jnp.einsum('gjtu,ugd->tgjd', attn_probs, keyval[..., HD:], precision=highest)
    return attended.reshape(LEN, QH * HD)

def layer(tokens, mix_gain, ffn_gain, ssm_gate, ssm_input, ssm_state, ssm_step, attn_query, attn_keyval, ssm_out, attn_out, ffn_gate, ffn_up, ffn_down, conv_input, conv_state, step_bias, decay_rate, segments):
    normed = low(rms_norm(tokens, mix_gain))
    gate_lin = low_back(product(normed, ssm_gate))
    mixer_in = low_back(low(jnp.concatenate([product(normed, ssm_input), product(normed, ssm_state)], axis=1)))
    step_lin = low_back(product(normed, ssm_step))
    queries = low_back(product(normed, attn_query))
    keyval = low_back(product(normed, attn_keyval.reshape(D, KVH * 2 * HD)))
    conv_taps = jnp.concatenate([conv_input, conv_state], axis=1)
    padded = jnp.pad(mixer_in.reshape(SEQ_ALL, LEN, DI + 2 * N), ((0, 0), (K - 1, 0), (0, 0)))
    conv_sum = padded[:, 0:LEN] * conv_taps[0]
    for tap_index in range(1, K):
        conv_sum = conv_sum + padded[:, tap_index:tap_index + LEN] * conv_taps[tap_index]
    activated = jax.nn.silu(conv_sum)
    step_size = jax.nn.softplus(step_lin + step_bias).reshape(SEQ_ALL, LEN, H)
    mixer_fn = jax.checkpoint(partial(sequence_mixer, decay_rate=decay_rate))
    ssm_result = lax.map(mixer_fn, (activated[..., :DI].reshape(SEQ_ALL, LEN, H, P_SIZE), activated[..., DI:DI + N], activated[..., DI + N:], step_size, segments))
    gated = low(ssm_result.reshape(SEQ_ALL * LEN, DI) * jax.nn.silu(gate_lin))
    cos_table, sin_table = rotary_tables(jnp.arange(LEN), HD)
    rotated_q = low(rotate(queries.reshape(SEQ_ALL, LEN, QH, HD), cos_table[:, None], sin_table[:, None]))
    kv_heads = keyval.reshape(SEQ_ALL, LEN, KVH, 2 * HD)
    rotated_kv = low(jnp.concatenate([rotate(kv_heads[..., :HD], cos_table[:, None], sin_table[:, None]), kv_heads[..., HD:]], axis=-1))
    attended = lax.map(jax.checkpoint(sequence_attention), (rotated_q, rotated_kv, segments))
    attended = low_back(low(attended.reshape(SEQ_ALL * LEN, QH * HD)))
    hidden = tokens + low_back(product(gated, ssm_out)) + low_back(product(attended, attn_out))
    normed_ffn = low(rms_norm(hidden, ffn_gain))
    gate_ffn = low_back(product(normed_ffn, ffn_gate))
    up_ffn = low_back(product(normed_ffn, ffn_up))
    act_ffn = low(jax.nn.silu(gate_ffn) * up_ffn)
    return hidden + low_back(product(act_ffn, ffn_down))

def reference(tokens, segments, cotangent, mix_gain, ffn_gain, ssm_gate, ssm_input, ssm_state, ssm_step, attn_query, attn_keyval, ssm_out, attn_out, ffn_gate, ffn_up, ffn_down, conv_input, conv_state, step_bias, decay_rate):
    primals = [tokens.reshape(SEQ_ALL * LEN, D), mix_gain, ffn_gain, ssm_gate, ssm_input, ssm_state, ssm_step, attn_query, attn_keyval, ssm_out, attn_out, ffn_gate, ffn_up, ffn_down, conv_input, conv_state, step_bias, decay_rate]
    primals = [argument.astype(jnp.float32) for argument in primals]
    result, pullback = jax.vjp(partial(layer, segments=segments), *primals)
    gradients = pullback(cotangent.reshape(SEQ_ALL * LEN, D).astype(jnp.float32))
    return (result.reshape(SEQ_ALL, LEN, D).astype(jnp.bfloat16), gradients[0].reshape(SEQ_ALL, LEN, D), gradients[1], gradients[2], gradients[3], gradients[4], gradients[5], gradients[6], gradients[7], gradients[8], gradients[9], gradients[10], gradients[11], gradients[12], gradients[13], gradients[14], gradients[15], gradients[16], gradients[17])
```

```python
import jax
import jax.numpy as jnp
from jax import lax
from jax.sharding import PartitionSpec as P

epsilon = 1e-05
highest = lax.Precision.HIGH


def shifted(block, axis, distance):
    devices = range(lax.axis_size(axis))
    route = [(i - distance, i) for i in devices if i - distance in devices]
    return lax.ppermute(block, axis, route)


def entering(value, axis, combine, identity, reverse):
    count, index = (lax.axis_size(axis), lax.axis_index(axis))
    everything = jax.tree.map(
        lambda part, kind: lax.all_gather(part.astype(kind), axis),
        value,
        (jnp.bfloat16, jnp.bfloat16),
    )
    start = jax.tree.map(
        lambda part, zero: jnp.broadcast_to(jnp.asarray(zero, part.dtype), part.shape),
        value,
        identity,
    )

    def step(k, before):
        at = count - 1 - k if reverse else k
        reached = at > index if reverse else at < index
        new = combine(
            before, jax.tree.map(lambda part, own: part[at].astype(own.dtype), everything, value)
        )
        return jax.tree.map(lambda a, b: jnp.where(reached, a, b), new, before)

    return lax.fori_loop(0, count, step, start)


def matmul(left_side, right_side):
    return jnp.dot(left_side, right_side, preferred_element_type=jnp.float32)


def weight_grad(left_side, right_side):
    return lax.dot_general(
        left_side, right_side, (((0,), (0,)), ((), ())), preferred_element_type=jnp.float32
    )


def back_product(left_side, right_side):
    return lax.dot_general(
        left_side, right_side, (((1,), (1,)), ((), ())), preferred_element_type=jnp.float32
    )


def rotary_tables(positions, head_dim):
    half_dim = head_dim // 2
    frequency = 10000.0 ** (-2.0 * jnp.arange(half_dim, dtype=jnp.float32) / head_dim)
    angles = positions.astype(jnp.float32)[:, None] * frequency[None, :]
    return (jnp.cos(angles), jnp.sin(angles))


def rotate(values, cos_table, sin_table):
    half_dim = values.shape[-1] // 2
    first_half = values[..., :half_dim]
    second_half = values[..., half_dim:]
    return jnp.concatenate(
        [
            first_half * cos_table - second_half * sin_table,
            second_half * cos_table + first_half * sin_table,
        ],
        axis=-1,
    )


def rotate_back(grads_in, cos_table, sin_table):
    half_dim = grads_in.shape[-1] // 2
    first_half = grads_in[..., :half_dim]
    second_half = grads_in[..., half_dim:]
    return jnp.concatenate(
        [
            first_half * cos_table + second_half * sin_table,
            second_half * cos_table - first_half * sin_table,
        ],
        axis=-1,
    )


def span_states(inner_act, input_mat, step_size, decay_rate, seg_part, seg_before):
    cumulative = jnp.cumsum(-step_size * decay_rate, axis=1)
    at_end = (seg_part == seg_part[:, -1:])[..., None]
    tail_decay = jnp.where(at_end, jnp.exp(cumulative[:, -1:, :] - cumulative), 0.0)
    weighted = inner_act * (tail_decay * step_size)[..., None]
    states = jnp.einsum("stha,stn->shan", weighted, input_mat, precision=highest)
    linked = (seg_part[:, -1] == seg_before)[:, None]
    linkage = jnp.where(linked, jnp.exp(cumulative[:, -1, :]), 0.0)
    return (states, linkage, cumulative)


def span_outputs(
    inner_act, input_mat, output_mat, step_size, seg_part, seg_before, cumulative, incoming
):
    length = inner_act.shape[1]
    ordinal = jnp.arange(length)
    allowed = (seg_part[:, :, None] == seg_part[:, None, :]) & (
        ordinal[:, None] >= ordinal[None, :]
    )[None]
    allowed = allowed[..., None]
    spread = cumulative[:, :, None, :] - cumulative[:, None, :, :]
    decays = jnp.where(allowed, jnp.exp(jnp.where(allowed, spread, 0.0)), 0.0)
    intersection = jnp.einsum("stn,sun->stu", output_mat, input_mat, precision=highest)
    mixing = intersection[..., None] * decays * step_size[:, None, :, :]
    local_part = jnp.einsum("stuh,suha->stha", mixing, inner_act, precision=highest)
    entrance = jnp.where((seg_part == seg_before[:, None])[..., None], jnp.exp(cumulative), 0.0)
    carried = (
        jnp.einsum("shan,stn->stha", incoming, output_mat, precision=highest) * entrance[..., None]
    )
    return local_part + carried


def combine_state(earlier, later):
    return (earlier[0] * later[0], later[0][..., None, None] * earlier[1] + later[1])


def conv_back(grad_conv, padded, conv_taps):
    tap_count = conv_taps.shape[0]
    length = grad_conv.shape[1]
    tap_grads = []
    grad_padded = jnp.zeros(padded.shape, jnp.float32)
    for tap_index in range(tap_count):
        tap_grads.append(
            jnp.sum(grad_conv * padded[:, tap_index : tap_index + length], axis=(0, 1))
        )
        grad_padded = grad_padded + jnp.pad(
            grad_conv * conv_taps[tap_index],
            ((0, 0), (tap_index, tap_count - 1 - tap_index), (0, 0)),
        )
    return (jnp.stack(tap_grads), grad_padded)


def add_rim(grad_padded, from_next, tap_count):
    own_part = grad_padded[:, tap_count - 1 :]
    length = own_part.shape[1]
    return jnp.concatenate(
        [own_part[:, : length - tap_count + 1], own_part[:, length - tap_count + 1 :] + from_next],
        axis=1,
    )


def attend_mask(seg_row, seg_part, offset):
    query_pos = offset + jnp.arange(seg_part.shape[0])
    key_pos = jnp.arange(seg_row.shape[0])
    return (query_pos[:, None] >= key_pos[None, :]) & (seg_part[:, None] == seg_row[None, :])


def attend_scores(queries, keyval, seg_row, seg_part, offset):
    head_dim = keyval.shape[1] // 2
    scores = jnp.einsum(
        "tqd,ud->qtu", queries, keyval[:, :head_dim], preferred_element_type=jnp.float32
    ) * head_dim ** (-0.5)
    allowed = attend_mask(seg_row, seg_part, offset)
    return jnp.where(allowed[None], scores, -1e30)


def attend_forward(queries, keyval, seg_row, seg_part, offset):
    head_dim = keyval.shape[1] // 2
    scores = attend_scores(queries, keyval, seg_row, seg_part, offset)
    largest = jnp.max(scores, axis=-1, keepdims=True)
    log_total = largest + jnp.log(jnp.sum(jnp.exp(scores - largest), axis=-1, keepdims=True))
    attn_probs = jnp.exp(scores - log_total).astype(jnp.bfloat16)
    attended = jnp.einsum(
        "qtu,ud->tqd", attn_probs, keyval[:, head_dim:], preferred_element_type=jnp.float32
    )
    return (attended, log_total)


def attend_backward(queries, keyval, seg_row, seg_part, log_total, grad_out, offset):
    head_dim = keyval.shape[1] // 2
    scale_factor = head_dim ** (-0.5)
    scores = attend_scores(queries, keyval, seg_row, seg_part, offset)
    attn_probs = jnp.exp(scores - log_total)
    probs_low = attn_probs.astype(jnp.bfloat16)
    grad_probs = jnp.einsum(
        "tqd,ud->qtu", grad_out, keyval[:, head_dim:], preferred_element_type=jnp.float32
    )
    inner_sum = jnp.sum(grad_probs * attn_probs, axis=-1, keepdims=True)
    grad_scores = (attn_probs * (grad_probs - inner_sum)).astype(jnp.bfloat16)
    grad_query = (
        jnp.einsum(
            "qtu,ud->tqd", grad_scores, keyval[:, :head_dim], preferred_element_type=jnp.float32
        )
        * scale_factor
    )
    grad_keys = (
        jnp.einsum("qtu,tqd->ud", grad_scores, queries, preferred_element_type=jnp.float32)
        * scale_factor
    )
    grad_vals = jnp.einsum("qtu,tqd->ud", probs_low, grad_out, preferred_element_type=jnp.float32)
    return (grad_query, jnp.concatenate([grad_keys, grad_vals], axis=1))


def gather_rows(parts):
    return lax.all_gather(jnp.concatenate(parts, axis=1), ("shard", "ctx"), axis=0, tiled=True)


def scatter_rows(parts):
    whole = jnp.concatenate([part.astype(jnp.bfloat16) for part in parts], axis=1)
    return lax.psum_scatter(whole, ("shard", "ctx"), scatter_dimension=0, tiled=True).astype(
        jnp.float32
    )


def split_columns(whole, widths):
    parts, start = ([], 0)
    for width in widths:
        parts.append(whole[:, start : start + width])
        start += width
    return parts


def fetch_keys(keyval_low):
    return lax.all_gather(keyval_low, "ctx", axis=1, tiled=True)


def shards(
    tokens,
    segments,
    cotangent,
    mix_gain,
    ffn_gain,
    ssm_gate,
    ssm_input,
    ssm_state,
    ssm_step,
    attn_query,
    attn_keyval,
    ssm_out,
    attn_out,
    ffn_gate,
    ffn_up,
    ffn_down,
    conv_input,
    conv_state,
    step_bias,
    decay_rate,
):
    seq_count, span_len, model_width = tokens.shape
    row_count = seq_count * span_len
    local_heads = step_bias.shape[0]
    inner_width = conv_input.shape[1]
    head_size = inner_width // local_heads
    state_width = conv_state.shape[1] // 2
    tap_count = conv_input.shape[0]
    head_dim = attn_keyval.shape[2] // 2
    query_width = attn_query.shape[1]
    query_heads = query_width // head_dim
    offset = lax.axis_index("ctx") * span_len
    keyval_width = 2 * head_dim
    ffn_width = ffn_gate.shape[1]
    step_pad = -local_heads % 128
    mixer_in_weights = gather_rows(
        [
            ssm_gate,
            ssm_input,
            ssm_state,
            attn_query,
            attn_keyval.reshape(-1, keyval_width),
            jnp.pad(ssm_step, ((0, 0), (0, step_pad))),
        ]
    )
    mixer_in_widths = (
        inner_width,
        inner_width,
        2 * state_width,
        query_width,
        keyval_width,
        local_heads + step_pad,
    )
    mixer_out_weights = gather_rows([ssm_out.T, attn_out.T])
    ffn_in_weights = gather_rows([ffn_gate, ffn_up])
    ffn_out_weights = gather_rows([ffn_down.T])
    inputs = tokens.reshape(row_count, model_width).astype(jnp.float32)
    inv_rms = lax.rsqrt(jnp.mean(inputs * inputs, axis=1, keepdims=True) + epsilon)
    normed = (inputs * inv_rms * mix_gain).astype(jnp.bfloat16)
    gate_lin, input_lin, state_lin, queries, keyval, step_wide = split_columns(
        matmul(normed, mixer_in_weights), mixer_in_widths
    )
    mixer_low = jnp.concatenate([input_lin, state_lin], axis=1).astype(jnp.bfloat16)
    mixer_low = mixer_low.reshape(seq_count, span_len, inner_width + 2 * state_width)
    step_lin = step_wide[:, :local_heads]
    rim_rows = shifted(mixer_low[:, span_len - tap_count + 1 :], "ctx", 1)
    padded = jnp.concatenate([rim_rows, mixer_low], axis=1).astype(jnp.float32)
    conv_taps = jnp.concatenate([conv_input, conv_state], axis=1)
    conv_sum = padded[:, 0:span_len] * conv_taps[0]
    for tap_index in range(1, tap_count):
        conv_sum = conv_sum + padded[:, tap_index : tap_index + span_len] * conv_taps[tap_index]
    activated = jax.nn.silu(conv_sum)
    inner_act = activated[..., :inner_width].reshape(seq_count, span_len, local_heads, head_size)
    input_mat = activated[..., inner_width : inner_width + state_width]
    output_mat = activated[..., inner_width + state_width :]
    step_size = jax.nn.softplus(step_lin + step_bias).reshape(seq_count, span_len, local_heads)
    seg_part = lax.dynamic_slice_in_dim(segments, offset, span_len, 1)
    seg_prior = lax.dynamic_slice_in_dim(segments, jnp.maximum(offset - 1, 0), 1, 1)[:, 0]
    seg_before = jnp.where(offset > 0, seg_prior, -1)
    states, linkage, cumulative = span_states(
        inner_act, input_mat, step_size, decay_rate, seg_part, seg_before
    )
    incoming = entering(
        (linkage, states),
        "ctx",
        combine_state,
        (jnp.ones_like(linkage), jnp.zeros_like(states)),
        False,
    )[1]

    def local_mixer(inner_arg, input_arg, output_arg, step_arg, rate_arg):
        states_new, linkage_new, cumulative_new = span_states(
            inner_arg, input_arg, step_arg, rate_arg, seg_part, seg_before
        )
        result = span_outputs(
            inner_arg,
            input_arg,
            output_arg,
            step_arg,
            seg_part,
            seg_before,
            cumulative_new,
            incoming,
        )
        return (result, states_new, linkage_new)

    mixer_values, mixer_pull = jax.vjp(
        local_mixer, inner_act, input_mat, output_mat, step_size, decay_rate
    )
    ssm_flat = mixer_values[0].reshape(row_count, inner_width)
    ssm_flat, ffn_in_weights = lax.optimization_barrier((ssm_flat, ffn_in_weights))
    gated = (ssm_flat * jax.nn.silu(gate_lin)).astype(jnp.bfloat16)
    cos_table, sin_table = rotary_tables(offset + jnp.arange(span_len), head_dim)
    rotated_q = rotate(
        queries.reshape(seq_count, span_len, query_heads, head_dim),
        cos_table[:, None],
        sin_table[:, None],
    ).astype(jnp.bfloat16)
    keyval_seq = keyval.reshape(seq_count, span_len, 2 * head_dim)
    keyval_low = jnp.concatenate(
        [rotate(keyval_seq[..., :head_dim], cos_table, sin_table), keyval_seq[..., head_dim:]],
        axis=-1,
    ).astype(jnp.bfloat16)
    all_keys = fetch_keys(keyval_low)

    def forward_one(sequence):
        return attend_forward(sequence[0], sequence[1], sequence[2], sequence[3], offset)

    attended, log_total = lax.map(forward_one, (rotated_q, all_keys, segments, seg_part))
    attended_low = attended.reshape(row_count, query_width).astype(jnp.bfloat16)
    mixed_low = jnp.concatenate([gated, attended_low], axis=1)
    mixer_sum = lax.psum(
        back_product(mixed_low, mixer_out_weights).astype(jnp.bfloat16), "tp"
    ).astype(jnp.float32)
    mixer_sum, ffn_out_weights = lax.optimization_barrier((mixer_sum, ffn_out_weights))
    hidden = inputs + mixer_sum
    inv_rms_ffn = lax.rsqrt(jnp.mean(hidden * hidden, axis=1, keepdims=True) + epsilon)
    normed_ffn = (hidden * inv_rms_ffn * ffn_gain).astype(jnp.bfloat16)
    gate_ffn, up_ffn = split_columns(matmul(normed_ffn, ffn_in_weights), (ffn_width, ffn_width))
    act_ffn = (jax.nn.silu(gate_ffn) * up_ffn).astype(jnp.bfloat16)
    ffn_result = lax.psum(back_product(act_ffn, ffn_out_weights).astype(jnp.bfloat16), "tp").astype(
        jnp.float32
    )
    layer_out = (hidden + ffn_result).astype(jnp.bfloat16).reshape(seq_count, span_len, model_width)
    grad_out = cotangent.reshape(row_count, model_width)
    grad_act = matmul(grad_out, ffn_out_weights)
    grad_ffndown = weight_grad(grad_out, act_ffn)
    sig_gate = jax.nn.sigmoid(gate_ffn)
    grad_up = (grad_act * gate_ffn * sig_gate).astype(jnp.bfloat16)
    grad_gate = (grad_act * up_ffn * sig_gate * (1.0 + gate_ffn * (1.0 - sig_gate))).astype(
        jnp.bfloat16
    )
    grad_ffn_low = jnp.concatenate([grad_gate, grad_up], axis=1)
    grad_ffnin = weight_grad(normed_ffn, grad_ffn_low)
    summed_ffn = scatter_rows([grad_ffnin, grad_ffndown])
    grad_normed_ffn = lax.psum(
        back_product(grad_ffn_low, ffn_in_weights).astype(jnp.bfloat16),
        "tp",
    ).astype(jnp.float32)
    grad_ffn_gain = jnp.sum(grad_normed_ffn * hidden * inv_rms_ffn, axis=0)
    scaled_ffn = grad_normed_ffn * ffn_gain
    grad_hidden = (
        grad_out.astype(jnp.float32)
        + inv_rms_ffn * scaled_ffn
        - hidden * inv_rms_ffn**3 * jnp.mean(scaled_ffn * hidden, axis=1, keepdims=True)
    )
    grad_hidden_low = grad_hidden.astype(jnp.bfloat16)
    summed_mixout = scatter_rows([weight_grad(grad_hidden_low, mixed_low)])
    grad_gated, grad_attended = split_columns(
        matmul(grad_hidden_low, mixer_out_weights), (inner_width, query_width)
    )
    grad_attended = grad_attended.astype(jnp.bfloat16).reshape(
        seq_count, span_len, query_heads, head_dim
    )
    sig_zeta = jax.nn.sigmoid(gate_lin)
    grad_ssm = (grad_gated * gate_lin * sig_zeta).reshape(
        seq_count, span_len, local_heads, head_size
    )
    grad_zeta = (grad_gated * ssm_flat * sig_zeta * (1.0 + gate_lin * (1.0 - sig_zeta))).astype(
        jnp.bfloat16
    )
    entrance = jnp.where((seg_part == seg_before[:, None])[..., None], jnp.exp(cumulative), 0.0)
    local_grad = jnp.einsum(
        "stha,stn->shan", grad_ssm * entrance[..., None], output_mat, precision=highest
    )
    later_grad = entering(
        (linkage, local_grad),
        "ctx",
        combine_state,
        (jnp.ones_like(linkage), jnp.zeros_like(local_grad)),
        True,
    )[1]
    grad_link = jnp.sum(later_grad * incoming, axis=(2, 3))
    grad_inner, grad_input_mat, grad_output_mat, grad_step, grad_decay_rate = mixer_pull(
        (grad_ssm, later_grad, grad_link)
    )
    grad_inner, grad_input_mat, grad_output_mat, grad_step, summed_ffn = lax.optimization_barrier(
        (grad_inner, grad_input_mat, grad_output_mat, grad_step, summed_ffn)
    )
    grad_step_lin = grad_step.reshape(row_count, local_heads) * jax.nn.sigmoid(step_lin + step_bias)
    grad_step_bias = jnp.sum(grad_step_lin, axis=0)
    grad_step_low = grad_step_lin.astype(jnp.bfloat16)
    grad_activated = jnp.concatenate(
        [grad_inner.reshape(seq_count, span_len, inner_width), grad_input_mat, grad_output_mat],
        axis=2,
    )
    sig_conv = jax.nn.sigmoid(conv_sum)
    grad_conv = grad_activated * sig_conv * (1.0 + conv_sum * (1.0 - sig_conv))
    grad_taps_inner, grad_pad_inner = conv_back(
        grad_conv[..., :inner_width], padded[..., :inner_width], conv_input
    )
    rim_inner = shifted(grad_pad_inner[:, : tap_count - 1].astype(jnp.bfloat16), "ctx", -1).astype(
        jnp.float32
    )
    grad_mixer_inner = (
        add_rim(grad_pad_inner, rim_inner, tap_count)
        .astype(jnp.bfloat16)
        .reshape(row_count, inner_width)
    )
    keys_back = fetch_keys(keyval_low)

    def backward_one(sequence):
        return attend_backward(
            sequence[0], sequence[1], sequence[2], sequence[3], sequence[4], sequence[5], offset
        )

    grad_rot_q, grad_keyval_all = lax.map(
        backward_one, (rotated_q, keys_back, segments, seg_part, log_total, grad_attended)
    )
    grad_keyval_rot = lax.psum_scatter(
        grad_keyval_all.astype(jnp.bfloat16), "ctx", scatter_dimension=1, tiled=True
    ).astype(jnp.float32)
    grad_queries = (
        rotate_back(grad_rot_q, cos_table[:, None], sin_table[:, None])
        .reshape(row_count, query_width)
        .astype(jnp.bfloat16)
    )
    grad_keyval_low = jnp.concatenate(
        [
            rotate_back(grad_keyval_rot[..., :head_dim], cos_table, sin_table),
            grad_keyval_rot[..., head_dim:],
        ],
        axis=-1,
    )
    grad_keyval_low = grad_keyval_low.reshape(row_count, 2 * head_dim).astype(jnp.bfloat16)
    gate_w, input_w, state_w, query_w, keyval_w, step_w = split_columns(
        mixer_in_weights, mixer_in_widths
    )
    grad_step_wide = jnp.pad(grad_step_low, ((0, 0), (0, step_pad)))
    grad_queries, grad_keyval_low, summed_mixout = lax.optimization_barrier(
        (grad_queries, grad_keyval_low, summed_mixout)
    )
    grad_norm_part = (
        back_product(grad_zeta, gate_w)
        + back_product(grad_mixer_inner, input_w)
        + back_product(grad_step_wide, step_w)
        + back_product(grad_queries, query_w)
        + back_product(grad_keyval_low, keyval_w)
    )
    grad_norm_sum, grad_conv_state = (
        lax.psum(grad_norm_part.astype(jnp.bfloat16), "tp").astype(jnp.float32),
        lax.psum(grad_conv[..., inner_width:].astype(jnp.bfloat16), "tp").astype(jnp.float32),
    )
    grad_taps_state, grad_pad_state = conv_back(
        grad_conv_state, padded[..., inner_width:], conv_state
    )
    rim_state = shifted(grad_pad_state[:, : tap_count - 1], "ctx", -1)
    grad_mixer_state = (
        add_rim(grad_pad_state, rim_state, tap_count)
        .astype(jnp.bfloat16)
        .reshape(row_count, 2 * state_width)
    )
    grad_normed = grad_norm_sum + back_product(grad_mixer_state, state_w)
    grad_mix_gain = jnp.sum(grad_normed * inputs * inv_rms, axis=0)
    scaled_mix = grad_normed * mix_gain
    grad_tokens = (
        grad_hidden
        + inv_rms * scaled_mix
        - inputs * inv_rms**3 * jnp.mean(scaled_mix * inputs, axis=1, keepdims=True)
    )
    grad_mixer_low = jnp.concatenate(
        [
            grad_zeta,
            grad_mixer_inner,
            grad_mixer_state,
            grad_queries,
            grad_keyval_low,
            grad_step_wide,
        ],
        axis=1,
    )
    summed_in = split_columns(
        scatter_rows([weight_grad(normed, grad_mixer_low)]), mixer_in_widths
    )
    summed_out = split_columns(summed_mixout, (inner_width, query_width))
    summed_gate, summed_up, summed_down = split_columns(summed_ffn, (ffn_width,) * 3)
    small_parts = (
        grad_taps_inner,
        grad_taps_state,
        grad_step_bias,
        grad_decay_rate,
        grad_mix_gain,
        grad_ffn_gain,
    )
    small_flat = jnp.concatenate([part.reshape(-1) for part in small_parts])
    small_flat = jnp.pad(small_flat, (0, -small_flat.shape[0] % 1024)).reshape(-1, 128)
    small_total = jnp.sum(lax.all_gather(small_flat, ("shard", "ctx")), axis=0).reshape(-1)
    small_sums, start = ([], 0)
    for part in small_parts:
        small_sums.append(small_total[start : start + part.size].reshape(part.shape))
        start += part.size
    return (
        layer_out,
        grad_tokens.reshape(seq_count, span_len, model_width),
        small_sums[4],
        small_sums[5],
        summed_in[0],
        summed_in[1],
        summed_in[2],
        summed_in[5][:, :local_heads],
        summed_in[3],
        summed_in[4].reshape(-1, 1, keyval_width),
        summed_out[0].T,
        summed_out[1].T,
        summed_gate,
        summed_up,
        summed_down.T,
        small_sums[0],
        small_sums[1],
        small_sums[2],
        small_sums[3],
    )


def solution(mesh):
    in_specs = (
        P("shard", "ctx", None),
        P("shard", None),
        P("shard", "ctx", None),
        P(),
        P(),
        P(("shard", "ctx"), "tp"),
        P(("shard", "ctx"), "tp"),
        P(("shard", "ctx"), None),
        P(("shard", "ctx"), "tp"),
        P(("shard", "ctx"), "tp"),
        P(("shard", "ctx"), "tp", None),
        P("tp", ("shard", "ctx")),
        P("tp", ("shard", "ctx")),
        P(("shard", "ctx"), "tp"),
        P(("shard", "ctx"), "tp"),
        P("tp", ("shard", "ctx")),
        P(None, "tp"),
        P(),
        P("tp"),
        P("tp"),
    )
    out_specs = (
        P("shard", "ctx", None),
        P("shard", "ctx", None),
        P(),
        P(),
        P(("shard", "ctx"), "tp"),
        P(("shard", "ctx"), "tp"),
        P(("shard", "ctx"), None),
        P(("shard", "ctx"), "tp"),
        P(("shard", "ctx"), "tp"),
        P(("shard", "ctx"), "tp", None),
        P("tp", ("shard", "ctx")),
        P("tp", ("shard", "ctx")),
        P(("shard", "ctx"), "tp"),
        P(("shard", "ctx"), "tp"),
        P("tp", ("shard", "ctx")),
        P(None, "tp"),
        P(),
        P("tp"),
        P("tp"),
    )
    return jax.shard_map(shards, mesh=mesh, in_specs=in_specs, out_specs=out_specs, check_vma=False)
```
